32 devices in a mesh: groups: 2 (over y), tm: 4 (over z), fibre: 4 (over x, core).
Axes of the slice: x: 2, y: 2, z: 4, core: 2. Of those that a mesh axis runs over, the one named last changes fastest.
Arguments:
- recording: bfloat16 [256, 128, 256], P(('groups', 'tm'), 'fibre'), parts along dimension 0, may hold values from -6 to 6
- conv_weight: bfloat16 [2, 3, 3, 256, 512], replicated, may hold values from -0.125 to 0.125
- conv_bias: float32 [2, 512], replicated, may hold values from -0.5 to 0.5
- res_weight: bfloat16 [2, 256, 256], replicated, may hold values from -0.375 to 0.375
- skip_weight: bfloat16 [2, 256, 256], replicated, may hold values from -0.375 to 0.375
- head_weight: bfloat16 [256, 1024], replicated, may hold values from -0.375 to 0.375
Outputs:
- residual_out: bfloat16 [256, 128, 256], P(('groups', 'tm'), 'fibre'), parts along dimension 0
- denoised: bfloat16 [256, 128, 1024], P(('groups', 'tm'), 'fibre'), parts along dimension 0
The draws below stay inside these ranges and needn't reach their ends.
There are 2 independent parts, one for each index of `groups`. The reference program is written for one: setup_inputs(seed, part) draws one part's arguments, and reference() takes and returns one part's arrays. A program takes and returns all parts, laid end to end along the dimension named above; an argument that names none is the same for every part. Nothing has to cross between parts.
All inputs are finite; a program needn't handle non-finite values.
Results may differ from the reference program's by a relative error of at most 0.0062.
Values may be sent and summed in bfloat16 or wider, within the bound.
A program may use at most 64 MiB of HBM per device.

```python
import jax
import jax.numpy as jnp

C = 256
PIX = 1024
LAYERS = 2
DILATION_SPAN = 32
TIME_PATCHES = 128
FIBRE_PATCHES = 128


def level_of(key, shape, pieces, low, high):
    def one(position, parts):
        draws = jax.random.uniform(jax.random.fold_in(jax.random.fold_in(key, 6), position), (parts,), jnp.float32, low / len(pieces), high / len(pieces))
        return jnp.repeat(jnp.exp(draws), shape[position] // parts).reshape((-1,) + (1,) * (len(shape) - position - 1))

    gain = one(*pieces[0])
    for cut in pieces[1:]:
        gain = gain * one(*cut)
    return gain


def noise(stream_key, dims, spread, reach, shards=(), kind=jnp.bfloat16):
    result = jax.random.normal(stream_key, dims, jnp.float32) * spread
    if len(shards) > 0:
        result = level_of(stream_key, dims, shards, -0.22, 0.18) * result
    return jnp.clip(result, min=-reach, max=reach).astype(kind)


def setup_inputs(seed: int = 0, part: int = 0) -> dict:
    streams_of = jax.random.split(jax.random.key(seed), 7)
    part_keys = jax.random.split(jax.random.fold_in(streams_of[6], part), 7)
    recording = noise(part_keys[0], (TIME_PATCHES, FIBRE_PATCHES, C), 1.0, 6.0, ((0, 4), (1, 4)))
    conv_weight = noise(streams_of[1], (LAYERS, 3, 3, C, 2 * C), (9 * C) ** -0.5, 0.125)
    conv_bias = jnp.clip(jax.random.uniform(streams_of[2], (LAYERS, 2 * C), jnp.float32, -0.5, 0.5), -0.5, 0.5)
    res_weight = noise(streams_of[3], (LAYERS, C, C), C ** -0.5, 0.375)
    skip_weight = noise(streams_of[4], (LAYERS, C, C), C ** -0.5, 0.375)
    head_weight = noise(streams_of[5], (C, PIX), C ** -0.5, 0.375)
    return {"recording": recording, "conv_weight": conv_weight, "conv_bias": conv_bias, "res_weight": res_weight, "skip_weight": skip_weight, "head_weight": head_weight}


def reference(recording, conv_weight, conv_bias, res_weight, skip_weight, head_weight):
    stream = recording
    skipped = jnp.zeros((TIME_PATCHES * FIBRE_PATCHES, C), jnp.float32)
    for layer in range(LAYERS):
        spacing = DILATION_SPAN * (2 ** layer)
        border_filled = jnp.pad(stream, ((spacing, spacing), (1, 1), (0, 0)))
        summed = jnp.zeros((TIME_PATCHES * FIBRE_PATCHES, 2 * C), jnp.float32)
        for time_offset in range(3):
            for fibre_offset in range(3):
                receptive_view = border_filled[time_offset * spacing:time_offset * spacing + TIME_PATCHES, fibre_offset:fibre_offset + FIBRE_PATCHES]
                summed = summed + jnp.dot(receptive_view.reshape(-1, C), conv_weight[layer, time_offset, fibre_offset], preferred_element_type=jnp.float32)
        before_gate = summed + conv_bias[layer]
        gated = (jnp.tanh(before_gate[:, :C]) * jax.nn.sigmoid(before_gate[:, C:])).astype(jnp.bfloat16)
        resident = stream.reshape(-1, C).astype(jnp.float32)
        stream = (resident + jnp.dot(gated, res_weight[layer], preferred_element_type=jnp.float32)).astype(jnp.bfloat16).reshape(TIME_PATCHES, FIBRE_PATCHES, C)
        skipped = skipped + jnp.dot(gated, skip_weight[layer], preferred_element_type=jnp.float32)
    rectified = jnp.maximum(skipped, 0.0).astype(jnp.bfloat16)
    denoised = jnp.dot(rectified, head_weight, preferred_element_type=jnp.float32).astype(jnp.bfloat16)
    return stream, denoised.reshape(TIME_PATCHES, FIBRE_PATCHES, PIX)
```

```python
import jax
import jax.numpy as jnp
from jax import lax
from jax.experimental import pallas as pl
from jax.experimental.pallas import tpu as pltpu
from jax.sharding import PartitionSpec as P

DILATION_SPAN = 32


def passed_along(shard, axis, by):
    devices = lax.axis_size(axis)
    pairs = [(i, i + by) for i in range(devices) if 0 <= i + by < devices]
    return lax.ppermute(shard, axis, pairs)


def padded(block, sides, width):
    for axis, dim in sides:
        count = lax.axis_size(axis)
        forward = [(i, i + 1) for i in range(count - 1)]
        backward = [(target, source) for source, target in forward]
        low = lax.ppermute(
            lax.slice_in_dim(block, block.shape[dim] - width, None, axis=dim), axis, forward
        )
        high = lax.ppermute(lax.slice_in_dim(block, 0, width, axis=dim), axis, backward)
        block = jnp.concatenate([low, block, high], axis=dim)
    return block


def gate_layer(earlier, middle, later, layer_weight, layer_bias):
    channels = middle.shape[-1]
    fibre_rows = middle.shape[-2] - 2
    summed = None
    for time_offset, block in enumerate((earlier, middle, later)):
        for fibre_offset in range(3):
            receptive_view = block[..., fibre_offset : fibre_offset + fibre_rows, :].reshape(
                -1, channels
            )
            product = jnp.dot(
                receptive_view,
                layer_weight[time_offset, fibre_offset],
                preferred_element_type=jnp.float32,
            )
            summed = product if summed is None else summed + product
    before_gate = summed + layer_bias
    return (jnp.tanh(before_gate[:, :channels]) * jax.nn.sigmoid(before_gate[:, channels:])).astype(
        jnp.bfloat16
    )


def update(gated, stream_rows, skipped, layer_res, layer_skip):
    new_stream = (
        stream_rows.astype(jnp.float32)
        + jnp.dot(gated, layer_res, preferred_element_type=jnp.float32)
    ).astype(jnp.bfloat16)
    new_skip = skipped + jnp.dot(gated, layer_skip, preferred_element_type=jnp.float32)
    return (new_stream, new_skip)


def head_out(skipped, head_weight):
    rectified = jnp.maximum(skipped, 0.0).astype(jnp.bfloat16)
    return jnp.dot(rectified, head_weight, preferred_element_type=jnp.float32).astype(jnp.bfloat16)


def local(recording, conv_weight, conv_bias, res_weight, skip_weight, head_weight):
    time_slices, strips, channels = recording.shape
    layer_count = conv_weight.shape[0]
    stream = recording
    skipped = jnp.zeros((time_slices * strips, channels), jnp.float32)
    for layer in range(layer_count):
        tap_spacing = DILATION_SPAN * 2**layer // time_slices
        earlier_bare = passed_along(stream, "tm", tap_spacing)
        later_bare = passed_along(stream, "tm", -tap_spacing)
        stacked = jnp.stack([earlier_bare, stream, later_bare])
        border_filled = padded(stacked, (("fibre", 2),), 1)
        earlier, middle, later = (border_filled[0], border_filled[1], border_filled[2])
        gated = gate_layer(earlier, middle, later, conv_weight[layer], conv_bias[layer])
        new_rows, skipped = update(
            gated, stream.reshape(-1, channels), skipped, res_weight[layer], skip_weight[layer]
        )
        stream = new_rows.reshape(time_slices, strips, channels)
    denoised = head_out(skipped, head_weight)
    return (stream, denoised.reshape(time_slices, strips, -1))


MESH = pl.DeviceIdType.MESH
M, O, I, F, S1M, S1F, S1I = range(7)
HALF = 16


def fused_kernel(x_ref, cw_hbm, cb_ref, rs_hbm, hd_hbm, res_ref, out_ref,
                 buf, cw, rs, hd, skip, w_sem, send_sem, recv_sem, hsend, hrecv):
    strips = x_ref.shape[1]
    channels = x_ref.shape[2]
    halves = x_ref.shape[0] // HALF
    rows = HALF * strips
    z = lax.axis_index("tm")
    f = lax.axis_index("fibre")
    fibres = lax.axis_size("fibre")
    is_mid = jnp.logical_or(z == 1, z == 2)
    is_end = jnp.logical_not(is_mid)
    toward = jnp.where(z < 2, 1, -1)
    inner = z + toward
    outer = jnp.clip(z - toward, 0, 3)
    tap_in = 1 + toward
    tap_out = 1 - toward
    has_low, has_high = f > 0, f < fibres - 1

    weight_copies = [
        pltpu.make_async_copy(cw_hbm.at[0], cw.at[0], w_sem.at[0]),
        pltpu.make_async_copy(rs_hbm, rs, w_sem.at[1]),
        pltpu.make_async_copy(cw_hbm.at[1], cw.at[1], w_sem.at[2]),
        pltpu.make_async_copy(hd_hbm, hd, w_sem.at[3]),
    ]
    for c in weight_copies:
        c.start()

    barrier = pltpu.get_barrier_semaphore()

    @pl.when(z > 0)
    def _():
        pl.semaphore_signal(barrier, inc=1, device_id={"tm": z - 1}, device_id_type=MESH)

    @pl.when(z < 3)
    def _():
        pl.semaphore_signal(barrier, inc=1, device_id={"tm": z + 1}, device_id_type=MESH)

    @pl.when(has_low)
    def _():
        pl.semaphore_signal(barrier, inc=1, device_id={"fibre": f - 1}, device_id_type=MESH)

    @pl.when(has_high)
    def _():
        pl.semaphore_signal(barrier, inc=1, device_id={"fibre": f + 1}, device_id_type=MESH)

    r_ids = lax.broadcasted_iota(jnp.int32, (rows, rows), 0)
    c_ids = lax.broadcasted_iota(jnp.int32, (rows, rows), 1)
    to_fibre_major = (
        (r_ids % HALF) * strips + r_ids // HALF == c_ids
    ).astype(jnp.float32).astype(jnp.bfloat16)
    to_time_major = (
        (c_ids % HALF) * strips + c_ids // HALF == r_ids
    ).astype(jnp.float32).astype(jnp.bfloat16)

    for h in range(halves):
        chunk = x_ref[h * HALF:(h + 1) * HALF].reshape(rows, channels)
        turned = jnp.dot(to_fibre_major, chunk, preferred_element_type=jnp.float32)
        buf[M, h, 1:strips + 1] = turned.astype(jnp.bfloat16).reshape(strips, HALF, channels)

    edge_zero = jnp.zeros((1, HALF, channels), jnp.bfloat16)

    @pl.when(jnp.logical_not(has_low))
    def _():
        for k in (M, O, I, F, S1M, S1F):
            for h in range(halves):
                buf[k, h, 0:1] = edge_zero

    @pl.when(jnp.logical_not(has_high))
    def _():
        for k in (M, O, I, F, S1M, S1F):
            for h in range(halves):
                buf[k, h, strips + 1:strips + 2] = edge_zero

    pl.semaphore_wait(
        barrier,
        (z > 0).astype(jnp.int32) + (z < 3).astype(jnp.int32)
        + has_low.astype(jnp.int32) + has_high.astype(jnp.int32),
    )

    def block_copy(src, dst, h, kind, to):
        return pltpu.make_async_remote_copy(
            src_ref=buf.at[src, h, pl.ds(1, strips)],
            dst_ref=buf.at[dst, h, pl.ds(1, strips)],
            send_sem=send_sem.at[kind, h],
            recv_sem=recv_sem.at[dst, h],
            device_id={"tm": to},
            device_id_type=MESH,
        )

    def arrived(dst, h):
        block_copy(dst, dst, h, 0, inner).wait_recv()

    def halo_low(k, h):
        return pltpu.make_async_remote_copy(
            src_ref=buf.at[k, h, pl.ds(1, 1)],
            dst_ref=buf.at[k, h, pl.ds(strips + 1, 1)],
            send_sem=hsend.at[k, h, 0],
            recv_sem=hrecv.at[k, h, 0],
            device_id={"fibre": f - 1},
            device_id_type=MESH,
        )

    def halo_high(k, h):
        return pltpu.make_async_remote_copy(
            src_ref=buf.at[k, h, pl.ds(strips, 1)],
            dst_ref=buf.at[k, h, pl.ds(0, 1)],
            send_sem=hsend.at[k, h, 1],
            recv_sem=hrecv.at[k, h, 1],
            device_id={"fibre": f + 1},
            device_id_type=MESH,
        )

    def halo_start(k, h):
        @pl.when(has_low)
        def _():
            halo_low(k, h).start()

        @pl.when(has_high)
        def _():
            halo_high(k, h).start()

    def halo_wait(k, h):
        @pl.when(has_high)
        def _():
            halo_low(k, h).wait_recv()

        @pl.when(has_low)
        def _():
            halo_high(k, h).wait_recv()

    def halo_drain(k, h):
        @pl.when(has_low)
        def _():
            halo_low(k, h).wait_send()

        @pl.when(has_high)
        def _():
            halo_high(k, h).wait_send()

    def gate(layer, taps, h):
        total = cb_ref[layer]
        for k, tap in taps:
            views = [
                buf[k, h, b:b + strips].reshape(rows, channels) for b in range(3)
            ]
            total = total + jnp.dot(
                jnp.concatenate(views, axis=1), cw[layer, tap],
                preferred_element_type=jnp.float32,
            )
        return (
            jnp.tanh(total[:, :channels]) * jax.nn.sigmoid(total[:, channels:])
        ).astype(jnp.bfloat16)

    def first_layer(dst, centre, taps, h, own):
        gated = gate(0, taps, h)
        base = buf[centre, h, 1:strips + 1].reshape(rows, channels).astype(jnp.float32)
        stream = base + jnp.dot(gated, rs[0, 0], preferred_element_type=jnp.float32)
        buf[dst, h, 1:strips + 1] = stream.astype(jnp.bfloat16).reshape(strips, HALF, channels)
        if own:
            skip[h] = jnp.dot(gated, rs[1, 0], preferred_element_type=jnp.float32)

    def last_layer(h):
        gated = gate(1, ((S1M, 1), (S1F, tap_in)), h)
        base = buf[S1M, h, 1:strips + 1].reshape(rows, channels).astype(jnp.float32)
        stream = (
            base + jnp.dot(gated, rs[0, 1], preferred_element_type=jnp.float32)
        ).astype(jnp.bfloat16)
        total = skip[h] + jnp.dot(gated, rs[1, 1], preferred_element_type=jnp.float32)
        both = jnp.concatenate(
            [stream, jnp.maximum(total, 0.0).astype(jnp.bfloat16)], axis=1
        )
        both = jnp.dot(
            to_time_major, both, preferred_element_type=jnp.float32
        ).astype(jnp.bfloat16)
        res_ref[h * HALF:(h + 1) * HALF] = both[:, :channels].reshape(HALF, strips, channels)
        out_ref[h * HALF:(h + 1) * HALF] = jnp.dot(
            both[:, channels:], hd[...], preferred_element_type=jnp.float32
        ).astype(jnp.bfloat16).reshape(HALF, strips, -1)

    @pl.when(is_mid)
    def _():
        block_copy(M, I, 0, 0, inner).start()
        block_copy(M, I, 0, 1, outer).start()
        for h in range(halves):
            halo_start(M, h)
        block_copy(M, I, 1, 1, outer).start()
        arrived(O, 0)
        block_copy(O, F, 0, 2, inner).start()
        block_copy(M, I, 1, 0, inner).start()
        halo_start(O, 0)
        arrived(I, 0)
        halo_start(I, 0)
        halo_wait(M, 0)
        halo_wait(O, 0)
        halo_wait(I, 0)
        weight_copies[0].wait()
        weight_copies[1].wait()
        own_taps = ((O, tap_out), (M, 1), (I, tap_in))
        first_layer(S1M, M, own_taps, 0, True)
        halo_start(S1M, 0)
        arrived(O, 1)
        block_copy(O, F, 1, 2, inner).start()
        halo_start(O, 1)
        arrived(F, 0)
        halo_start(F, 0)
        halo_wait(F, 0)
        inner_taps = ((M, tap_out), (I, 1), (F, tap_in))
        first_layer(S1I, I, inner_taps, 0, False)
        block_copy(S1I, S1F, 0, 3, outer).start()
        far_taps = ((I, tap_out), (F, 1))
        first_layer(S1F, F, far_taps, 0, False)
        halo_start(S1F, 0)
        arrived(I, 1)
        halo_start(I, 1)
        halo_wait(M, 1)
        halo_wait(O, 1)
        halo_wait(I, 1)
        first_layer(S1M, M, own_taps, 1, True)
        halo_start(S1M, 1)
        halo_wait(S1M, 0)
        halo_wait(S1F, 0)
        weight_copies[2].wait()
        weight_copies[3].wait()
        last_layer(0)
        arrived(F, 1)
        halo_start(F, 1)
        halo_wait(F, 1)
        first_layer(S1I, I, inner_taps, 1, False)
        block_copy(S1I, S1F, 1, 3, outer).start()
        first_layer(S1F, F, far_taps, 1, False)
        halo_start(S1F, 1)
        halo_wait(S1M, 1)
        halo_wait(S1F, 1)
        last_layer(1)
        for h in range(halves):
            block_copy(M, I, h, 0, inner).wait_send()
            block_copy(M, I, h, 1, outer).wait_send()
            block_copy(O, F, h, 2, inner).wait_send()
            block_copy(S1I, S1F, h, 3, outer).wait_send()
            for k in (O, F):
                halo_drain(k, h)

    @pl.when(is_end)
    def _():
        for h in range(halves):
            block_copy(M, O, h, 0, inner).start()
        for h in range(halves):
            halo_start(M, h)
        weight_copies[0].wait()
        weight_copies[1].wait()
        for h in range(halves):
            arrived(I, h)
            halo_start(I, h)
            halo_wait(M, h)
            halo_wait(I, h)
            first_layer(S1M, M, ((M, 1), (I, tap_in)), h, True)
            halo_start(S1M, h)
        weight_copies[2].wait()
        weight_copies[3].wait()
        for h in range(halves):
            arrived(S1F, h)
            halo_start(S1F, h)
            halo_wait(S1M, h)
            halo_wait(S1F, h)
            last_layer(h)
        for h in range(halves):
            block_copy(M, O, h, 0, inner).wait_send()

    for h in range(halves):
        for k in (M, I, S1M, S1F):
            halo_drain(k, h)


def fused(recording, conv_weight, conv_bias, res_weight, skip_weight, head_weight):
    times, strips, channels = recording.shape
    layers = conv_weight.shape[0]
    halves = times // HALF
    pixels = head_weight.shape[1]
    vmem = pl.BlockSpec(memory_space=pltpu.VMEM)
    hbm = pl.BlockSpec(memory_space=pl.ANY)
    weights = conv_weight.reshape(layers, 3, 3 * channels, 2 * channels)
    sides = jnp.stack([res_weight, skip_weight])
    return pl.pallas_call(
        fused_kernel,
        out_shape=(
            jax.ShapeDtypeStruct((times, strips, channels), jnp.bfloat16),
            jax.ShapeDtypeStruct((times, strips, pixels), jnp.bfloat16),
        ),
        in_specs=[vmem, hbm, vmem, hbm, hbm],
        out_specs=(vmem, vmem),
        scratch_shapes=[
            pltpu.VMEM((7, halves, strips + 2, HALF, channels), jnp.bfloat16),
            pltpu.VMEM(weights.shape, jnp.bfloat16),
            pltpu.VMEM(sides.shape, jnp.bfloat16),
            pltpu.VMEM(head_weight.shape, jnp.bfloat16),
            pltpu.VMEM((halves, HALF * strips, channels), jnp.float32),
            pltpu.SemaphoreType.DMA((4,)),
            pltpu.SemaphoreType.DMA((4, halves)),
            pltpu.SemaphoreType.DMA((7, halves)),
            pltpu.SemaphoreType.DMA((7, halves, 2)),
            pltpu.SemaphoreType.DMA((7, halves, 2)),
        ],
        compiler_params=pltpu.CompilerParams(
            collective_id=0, has_side_effects=True, vmem_limit_bytes=56 * 2**20
        ),
        cost_estimate=pl.CostEstimate(
            flops=10**10, bytes_accessed=10**7, transcendentals=10**6
        ),
    )(recording, weights, conv_bias.reshape(layers, 1, -1), sides, head_weight)


def program(recording, conv_weight, *rest):
    four = lax.axis_size("tm") == 4
    if four and recording.shape[0] == DILATION_SPAN and conv_weight.shape[0] == 2:
        return fused(recording, conv_weight, *rest)
    return local(recording, conv_weight, *rest)


def solution(mesh):
    return jax.shard_map(
        program,
        mesh=mesh,
        in_specs=(P(("groups", "tm"), "fibre", None), P(), P(), P(), P(), P()),
        out_specs=(P(("groups", "tm"), "fibre", None), P(("groups", "tm"), "fibre", None)),
        check_vma=False,
    )
```

```python
import jax
import jax.numpy as jnp
from jax import lax
from jax.experimental import pallas as pl
from jax.experimental.pallas import tpu as pltpu
from jax.sharding import PartitionSpec as P

DILATION_SPAN = 32


def passed_along(shard, axis, by):
    devices = lax.axis_size(axis)
    pairs = [(i, i + by) for i in range(devices) if 0 <= i + by < devices]
    return lax.ppermute(shard, axis, pairs)


def padded(block, sides, width):
    for axis, dim in sides:
        count = lax.axis_size(axis)
        forward = [(i, i + 1) for i in range(count - 1)]
        backward = [(target, source) for source, target in forward]
        low = lax.ppermute(
            lax.slice_in_dim(block, block.shape[dim] - width, None, axis=dim), axis, forward
        )
        high = lax.ppermute(lax.slice_in_dim(block, 0, width, axis=dim), axis, backward)
        block = jnp.concatenate([low, block, high], axis=dim)
    return block


def gate_layer(earlier, middle, later, layer_weight, layer_bias):
    channels = middle.shape[-1]
    fibre_rows = middle.shape[-2] - 2
    summed = None
    for time_offset, block in enumerate((earlier, middle, later)):
        for fibre_offset in range(3):
            receptive_view = block[..., fibre_offset : fibre_offset + fibre_rows, :].reshape(
                -1, channels
            )
            product = jnp.dot(
                receptive_view,
                layer_weight[time_offset, fibre_offset],
                preferred_element_type=jnp.float32,
            )
            summed = product if summed is None else summed + product
    before_gate = summed + layer_bias
    return (jnp.tanh(before_gate[:, :channels]) * jax.nn.sigmoid(before_gate[:, channels:])).astype(
        jnp.bfloat16
    )


def update(gated, stream_rows, skipped, layer_res, layer_skip):
    new_stream = (
        stream_rows.astype(jnp.float32)
        + jnp.dot(gated, layer_res, preferred_element_type=jnp.float32)
    ).astype(jnp.bfloat16)
    new_skip = skipped + jnp.dot(gated, layer_skip, preferred_element_type=jnp.float32)
    return (new_stream, new_skip)


def head_out(skipped, head_weight):
    rectified = jnp.maximum(skipped, 0.0).astype(jnp.bfloat16)
    return jnp.dot(rectified, head_weight, preferred_element_type=jnp.float32).astype(jnp.bfloat16)


def local(recording, conv_weight, conv_bias, res_weight, skip_weight, head_weight):
    time_slices, strips, channels = recording.shape
    layer_count = conv_weight.shape[0]
    stream = recording
    skipped = jnp.zeros((time_slices * strips, channels), jnp.float32)
    for layer in range(layer_count):
        tap_spacing = DILATION_SPAN * 2**layer // time_slices
        earlier_bare = passed_along(stream, "tm", tap_spacing)
        later_bare = passed_along(stream, "tm", -tap_spacing)
        stacked = jnp.stack([earlier_bare, stream, later_bare])
        border_filled = padded(stacked, (("fibre", 2),), 1)
        earlier, middle, later = (border_filled[0], border_filled[1], border_filled[2])
        gated = gate_layer(earlier, middle, later, conv_weight[layer], conv_bias[layer])
        new_rows, skipped = update(
            gated, stream.reshape(-1, channels), skipped, res_weight[layer], skip_weight[layer]
        )
        stream = new_rows.reshape(time_slices, strips, channels)
    denoised = head_out(skipped, head_weight)
    return (stream, denoised.reshape(time_slices, strips, -1))


MESH = pl.DeviceIdType.MESH
M, O, I, F, S1M, S1F, S1I = range(7)
HALF = 16


def fused_kernel(x_hbm, cw_hbm, cb_hbm, rw_hbm, sw_hbm, stream_ref, rect_ref,
                 x_ref, cb_ref, buf, cw, rw, sw, skip, w_sem, send_sem, recv_sem, hsend, hrecv):
    x_copy = pltpu.make_async_copy(x_hbm, x_ref, w_sem.at[4])
    x_copy.start()
    strips = x_ref.shape[1]
    channels = x_ref.shape[2]
    halves = x_ref.shape[0] // HALF
    rows = HALF * strips
    z = lax.axis_index("tm")
    f = lax.axis_index("fibre")
    fibres = lax.axis_size("fibre")
    is_mid = jnp.logical_or(z == 1, z == 2)
    is_end = jnp.logical_not(is_mid)
    toward = jnp.where(z < 2, 1, -1)
    inner = z + toward
    outer = jnp.clip(z - toward, 0, 3)
    tap_in = 1 + toward
    tap_out = 1 - toward
    has_low, has_high = f > 0, f < fibres - 1

    weight_copies = [
        pltpu.make_async_copy(cw_hbm.at[0], cw.at[0], w_sem.at[0]),
        pltpu.make_async_copy(rw_hbm, rw, w_sem.at[1]),
        pltpu.make_async_copy(cw_hbm.at[1], cw.at[1], w_sem.at[2]),
        pltpu.make_async_copy(sw_hbm, sw, w_sem.at[3]),
        pltpu.make_async_copy(cb_hbm, cb_ref, w_sem.at[5]),
    ]
    for c in weight_copies:
        c.start()

    barrier = pltpu.get_barrier_semaphore()

    @pl.when(z > 0)
    def _():
        pl.semaphore_signal(barrier, inc=1, device_id={"tm": z - 1}, device_id_type=MESH)

    @pl.when(z < 3)
    def _():
        pl.semaphore_signal(barrier, inc=1, device_id={"tm": z + 1}, device_id_type=MESH)

    @pl.when(has_low)
    def _():
        pl.semaphore_signal(barrier, inc=1, device_id={"fibre": f - 1}, device_id_type=MESH)

    @pl.when(has_high)
    def _():
        pl.semaphore_signal(barrier, inc=1, device_id={"fibre": f + 1}, device_id_type=MESH)

    r_ids = lax.broadcasted_iota(jnp.int32, (rows, rows), 0)
    c_ids = lax.broadcasted_iota(jnp.int32, (rows, rows), 1)
    to_fibre_major = (
        (r_ids % HALF) * strips + r_ids // HALF == c_ids
    ).astype(jnp.float32).astype(jnp.bfloat16)

    x_copy.wait()
    for h in range(halves):
        chunk = x_ref[h * HALF:(h + 1) * HALF].reshape(rows, channels)
        turned = jnp.dot(to_fibre_major, chunk, preferred_element_type=jnp.float32)
        buf[M, h, 1:strips + 1] = turned.astype(jnp.bfloat16).reshape(strips, HALF, channels)

    edge_zero = jnp.zeros((1, HALF, channels), jnp.bfloat16)

    @pl.when(jnp.logical_not(has_low))
    def _():
        for k in (M, O, I, F, S1M, S1F):
            for h in range(halves):
                buf[k, h, 0:1] = edge_zero

    @pl.when(jnp.logical_not(has_high))
    def _():
        for k in (M, O, I, F, S1M, S1F):
            for h in range(halves):
                buf[k, h, strips + 1:strips + 2] = edge_zero

    pl.semaphore_wait(
        barrier,
        (z > 0).astype(jnp.int32) + (z < 3).astype(jnp.int32)
        + has_low.astype(jnp.int32) + has_high.astype(jnp.int32),
    )

    def block_copy(src, dst, h, kind, to):
        return pltpu.make_async_remote_copy(
            src_ref=buf.at[src, h, pl.ds(1, strips)],
            dst_ref=buf.at[dst, h, pl.ds(1, strips)],
            send_sem=send_sem.at[kind, h],
            recv_sem=recv_sem.at[dst, h],
            device_id={"tm": to},
            device_id_type=MESH,
        )

    def arrived(dst, h):
        block_copy(dst, dst, h, 0, inner).wait_recv()

    def halo_low(k, h):
        return pltpu.make_async_remote_copy(
            src_ref=buf.at[k, h, pl.ds(1, 1)],
            dst_ref=buf.at[k, h, pl.ds(strips + 1, 1)],
            send_sem=hsend.at[k, h, 0],
            recv_sem=hrecv.at[k, h, 0],
            device_id={"fibre": f - 1},
            device_id_type=MESH,
        )

    def halo_high(k, h):
        return pltpu.make_async_remote_copy(
            src_ref=buf.at[k, h, pl.ds(strips, 1)],
            dst_ref=buf.at[k, h, pl.ds(0, 1)],
            send_sem=hsend.at[k, h, 1],
            recv_sem=hrecv.at[k, h, 1],
            device_id={"fibre": f + 1},
            device_id_type=MESH,
        )

    def halo_start(k, h):
        @pl.when(has_low)
        def _():
            halo_low(k, h).start()

        @pl.when(has_high)
        def _():
            halo_high(k, h).start()

    def halo_wait(k, h):
        @pl.when(has_high)
        def _():
            halo_low(k, h).wait_recv()

        @pl.when(has_low)
        def _():
            halo_high(k, h).wait_recv()

    def halo_drain(k, h):
        @pl.when(has_low)
        def _():
            halo_low(k, h).wait_send()

        @pl.when(has_high)
        def _():
            halo_high(k, h).wait_send()

    def gate(layer, taps, h):
        total = cb_ref[layer:layer + 1]
        for k, tap in taps:
            views = [
                buf[k, h, b:b + strips].reshape(rows, channels) for b in range(3)
            ]
            total = total + jnp.dot(
                jnp.concatenate(views, axis=1), cw[layer, tap],
                preferred_element_type=jnp.float32,
            )
        return (
            jnp.tanh(total[:, :channels]) * jax.nn.sigmoid(total[:, channels:])
        ).astype(jnp.bfloat16)

    def first_layer(dst, centre, taps, h, own):
        gated = gate(0, taps, h)
        base = buf[centre, h, 1:strips + 1].reshape(rows, channels).astype(jnp.float32)
        stream = base + jnp.dot(gated, rw[0], preferred_element_type=jnp.float32)
        buf[dst, h, 1:strips + 1] = stream.astype(jnp.bfloat16).reshape(strips, HALF, channels)
        if own:
            skip[h] = jnp.dot(gated, sw[0], preferred_element_type=jnp.float32)

    def last_layer(h):
        gated = gate(1, ((S1M, 1), (S1F, tap_in)), h)
        base = buf[S1M, h, 1:strips + 1].reshape(rows, channels).astype(jnp.float32)
        stream = base + jnp.dot(gated, rw[1], preferred_element_type=jnp.float32)
        stream_ref[h] = stream.astype(jnp.bfloat16)
        total = skip[h] + jnp.dot(gated, sw[1], preferred_element_type=jnp.float32)
        rect_ref[h] = jnp.maximum(total, 0.0).astype(jnp.bfloat16)

    @pl.when(is_mid)
    def _():
        block_copy(M, I, 0, 0, inner).start()
        block_copy(M, I, 0, 1, outer).start()
        for h in range(halves):
            halo_start(M, h)
        block_copy(M, I, 1, 1, outer).start()
        arrived(O, 0)
        block_copy(O, F, 0, 2, inner).start()
        block_copy(M, I, 1, 0, inner).start()
        halo_start(O, 0)
        arrived(I, 0)
        halo_start(I, 0)
        halo_wait(M, 0)
        halo_wait(O, 0)
        halo_wait(I, 0)
        weight_copies[0].wait()
        weight_copies[1].wait()
        weight_copies[3].wait()
        weight_copies[4].wait()
        own_taps = ((O, tap_out), (M, 1), (I, tap_in))
        first_layer(S1M, M, own_taps, 0, True)
        halo_start(S1M, 0)
        arrived(O, 1)
        block_copy(O, F, 1, 2, inner).start()
        halo_start(O, 1)
        arrived(F, 0)
        halo_start(F, 0)
        halo_wait(F, 0)
        inner_taps = ((M, tap_out), (I, 1), (F, tap_in))
        first_layer(S1I, I, inner_taps, 0, False)
        block_copy(S1I, S1F, 0, 3, outer).start()
        far_taps = ((I, tap_out), (F, 1))
        first_layer(S1F, F, far_taps, 0, False)
        halo_start(S1F, 0)
        arrived(I, 1)
        halo_start(I, 1)
        halo_wait(M, 1)
        halo_wait(O, 1)
        halo_wait(I, 1)
        first_layer(S1M, M, own_taps, 1, True)
        halo_start(S1M, 1)
        halo_wait(S1M, 0)
        halo_wait(S1F, 0)
        weight_copies[2].wait()
        last_layer(0)
        arrived(F, 1)
        halo_start(F, 1)
        halo_wait(F, 1)
        first_layer(S1I, I, inner_taps, 1, False)
        block_copy(S1I, S1F, 1, 3, outer).start()
        first_layer(S1F, F, far_taps, 1, False)
        halo_start(S1F, 1)
        halo_wait(S1M, 1)
        halo_wait(S1F, 1)
        last_layer(1)
        for h in range(halves):
            block_copy(M, I, h, 0, inner).wait_send()
            block_copy(M, I, h, 1, outer).wait_send()
            block_copy(O, F, h, 2, inner).wait_send()
            block_copy(S1I, S1F, h, 3, outer).wait_send()
            for k in (O, F):
                halo_drain(k, h)

    @pl.when(is_end)
    def _():
        for h in range(halves):
            block_copy(M, O, h, 0, inner).start()
        for h in range(halves):
            halo_start(M, h)
        weight_copies[0].wait()
        weight_copies[1].wait()
        weight_copies[3].wait()
        weight_copies[4].wait()
        for h in range(halves):
            arrived(I, h)
            halo_start(I, h)
            halo_wait(M, h)
            halo_wait(I, h)
            first_layer(S1M, M, ((M, 1), (I, tap_in)), h, True)
            halo_start(S1M, h)
        weight_copies[2].wait()
        for h in range(halves):
            arrived(S1F, h)
            halo_start(S1F, h)
            halo_wait(S1M, h)
            halo_wait(S1F, h)
            last_layer(h)
        for h in range(halves):
            block_copy(M, O, h, 0, inner).wait_send()

    for h in range(halves):
        for k in (M, I, S1M, S1F):
            halo_drain(k, h)


def head_kernel(stream_ref, rect_ref, hd_ref, res_ref, out_ref):
    times, strips, channels = res_ref.shape
    rows = times * strips
    r_ids = lax.broadcasted_iota(jnp.int32, (rows, rows), 0)
    c_ids = lax.broadcasted_iota(jnp.int32, (rows, rows), 1)
    to_time_major = (
        (c_ids % HALF) * strips + c_ids // HALF == r_ids
    ).astype(jnp.float32).astype(jnp.bfloat16)

    def turned(block):
        return jnp.dot(
            to_time_major, block, preferred_element_type=jnp.float32
        ).astype(jnp.bfloat16)

    res_ref[...] = turned(stream_ref[0]).reshape(times, strips, channels)
    out_ref[...] = jnp.dot(
        turned(rect_ref[0]), hd_ref[...], preferred_element_type=jnp.float32
    ).astype(jnp.bfloat16).reshape(times, strips, -1)


def fused(recording, conv_weight, conv_bias, res_weight, skip_weight, head_weight):
    times, strips, channels = recording.shape
    layers = conv_weight.shape[0]
    halves = times // HALF
    rows = HALF * strips
    pixels = head_weight.shape[1]
    vmem = pl.BlockSpec(memory_space=pltpu.VMEM)
    hbm = pl.BlockSpec(memory_space=pl.ANY)
    weights = conv_weight.reshape(layers, 3, 3 * channels, 2 * channels)
    flat = jax.ShapeDtypeStruct((halves, rows, channels), jnp.bfloat16)
    stream, rectified = pl.pallas_call(
        fused_kernel,
        out_shape=(flat, flat),
        in_specs=[hbm] * 5,
        out_specs=(vmem, vmem),
        scratch_shapes=[
            pltpu.VMEM(recording.shape, jnp.bfloat16),
            pltpu.VMEM(conv_bias.shape, jnp.float32),
            pltpu.VMEM((7, halves, strips + 2, HALF, channels), jnp.bfloat16),
            pltpu.VMEM(weights.shape, jnp.bfloat16),
            pltpu.VMEM(res_weight.shape, jnp.bfloat16),
            pltpu.VMEM(skip_weight.shape, jnp.bfloat16),
            pltpu.VMEM((halves, rows, channels), jnp.float32),
            pltpu.SemaphoreType.DMA((6,)),
            pltpu.SemaphoreType.DMA((4, halves)),
            pltpu.SemaphoreType.DMA((7, halves)),
            pltpu.SemaphoreType.DMA((7, halves, 2)),
            pltpu.SemaphoreType.DMA((7, halves, 2)),
        ],
        compiler_params=pltpu.CompilerParams(
            collective_id=0, has_side_effects=True, vmem_limit_bytes=62 * 2**20
        ),
        cost_estimate=pl.CostEstimate(
            flops=10**10, bytes_accessed=10**7, transcendentals=10**6
        ),
    )(recording, weights, conv_bias, res_weight, skip_weight)
    block = pl.BlockSpec((1, rows, channels), lambda h: (h, 0, 0))
    return pl.pallas_call(
        head_kernel,
        grid=(halves,),
        out_shape=(
            jax.ShapeDtypeStruct((times, strips, channels), jnp.bfloat16),
            jax.ShapeDtypeStruct((times, strips, pixels), jnp.bfloat16),
        ),
        in_specs=[block, block, pl.BlockSpec((channels, pixels), lambda h: (0, 0))],
        out_specs=(
            pl.BlockSpec((HALF, strips, channels), lambda h: (h, 0, 0)),
            pl.BlockSpec((HALF, strips, pixels), lambda h: (h, 0, 0)),
        ),
        compiler_params=pltpu.CompilerParams(vmem_limit_bytes=62 * 2**20),
        cost_estimate=pl.CostEstimate(
            flops=10**9, bytes_accessed=4 * 10**6, transcendentals=0
        ),
    )(stream, rectified, head_weight)


def program(recording, conv_weight, *rest):
    four = lax.axis_size("tm") == 4
    if four and recording.shape[0] == DILATION_SPAN and conv_weight.shape[0] == 2:
        return fused(recording, conv_weight, *rest)
    return local(recording, conv_weight, *rest)


def solution(mesh):
    return jax.shard_map(
        program,
        mesh=mesh,
        in_specs=(P(("groups", "tm"), "fibre", None), P(), P(), P(), P(), P()),
        out_specs=(P(("groups", "tm"), "fibre", None), P(("groups", "tm"), "fibre", None)),
        check_vma=False,
    )
```

```python
import jax
import jax.numpy as jnp
from jax import lax
from jax.experimental import pallas as pl
from jax.experimental.pallas import tpu as pltpu
from jax.sharding import PartitionSpec as P

DILATION_SPAN = 32


def passed_along(shard, axis, by):
    devices = lax.axis_size(axis)
    pairs = [(i, i + by) for i in range(devices) if 0 <= i + by < devices]
    return lax.ppermute(shard, axis, pairs)


def padded(block, sides, width):
    for axis, dim in sides:
        count = lax.axis_size(axis)
        forward = [(i, i + 1) for i in range(count - 1)]
        backward = [(target, source) for source, target in forward]
        low = lax.ppermute(
            lax.slice_in_dim(block, block.shape[dim] - width, None, axis=dim), axis, forward
        )
        high = lax.ppermute(lax.slice_in_dim(block, 0, width, axis=dim), axis, backward)
        block = jnp.concatenate([low, block, high], axis=dim)
    return block


def gate_layer(earlier, middle, later, layer_weight, layer_bias):
    channels = middle.shape[-1]
    fibre_rows = middle.shape[-2] - 2
    summed = None
    for time_offset, block in enumerate((earlier, middle, later)):
        for fibre_offset in range(3):
            receptive_view = block[..., fibre_offset : fibre_offset + fibre_rows, :].reshape(
                -1, channels
            )
            product = jnp.dot(
                receptive_view,
                layer_weight[time_offset, fibre_offset],
                preferred_element_type=jnp.float32,
            )
            summed = product if summed is None else summed + product
    before_gate = summed + layer_bias
    return (jnp.tanh(before_gate[:, :channels]) * jax.nn.sigmoid(before_gate[:, channels:])).astype(
        jnp.bfloat16
    )


def update(gated, stream_rows, skipped, layer_res, layer_skip):
    new_stream = (
        stream_rows.astype(jnp.float32)
        + jnp.dot(gated, layer_res, preferred_element_type=jnp.float32)
    ).astype(jnp.bfloat16)
    new_skip = skipped + jnp.dot(gated, layer_skip, preferred_element_type=jnp.float32)
    return (new_stream, new_skip)


def head_out(skipped, head_weight):
    rectified = jnp.maximum(skipped, 0.0).astype(jnp.bfloat16)
    return jnp.dot(rectified, head_weight, preferred_element_type=jnp.float32).astype(jnp.bfloat16)


def local(recording, conv_weight, conv_bias, res_weight, skip_weight, head_weight):
    time_slices, strips, channels = recording.shape
    layer_count = conv_weight.shape[0]
    stream = recording
    skipped = jnp.zeros((time_slices * strips, channels), jnp.float32)
    for layer in range(layer_count):
        tap_spacing = DILATION_SPAN * 2**layer // time_slices
        earlier_bare = passed_along(stream, "tm", tap_spacing)
        later_bare = passed_along(stream, "tm", -tap_spacing)
        stacked = jnp.stack([earlier_bare, stream, later_bare])
        border_filled = padded(stacked, (("fibre", 2),), 1)
        earlier, middle, later = (border_filled[0], border_filled[1], border_filled[2])
        gated = gate_layer(earlier, middle, later, conv_weight[layer], conv_bias[layer])
        new_rows, skipped = update(
            gated, stream.reshape(-1, channels), skipped, res_weight[layer], skip_weight[layer]
        )
        stream = new_rows.reshape(time_slices, strips, channels)
    denoised = head_out(skipped, head_weight)
    return (stream, denoised.reshape(time_slices, strips, -1))


MESH = pl.DeviceIdType.MESH
M, O, I, F, S1M, S1F, S1I = range(7)
HALF = 16


def fused_kernel(x_hbm, cw_hbm, cb_hbm, rw_hbm, sw_hbm, stream_ref, rect_ref,
                 x_ref, cb_ref, buf, cw, rw, sw, skip, w_sem, send_sem, recv_sem, hsend, hrecv):
    x_copy = pltpu.make_async_copy(x_hbm, x_ref, w_sem.at[4])
    x_copy.start()
    strips = x_ref.shape[1]
    channels = x_ref.shape[2]
    halves = x_ref.shape[0] // HALF
    rows = HALF * strips
    z = lax.axis_index("tm")
    f = lax.axis_index("fibre")
    fibres = lax.axis_size("fibre")
    is_mid = jnp.logical_or(z == 1, z == 2)
    is_end = jnp.logical_not(is_mid)
    toward = jnp.where(z < 2, 1, -1)
    inner = z + toward
    outer = jnp.clip(z - toward, 0, 3)
    tap_in = 1 + toward
    tap_out = 1 - toward
    has_low, has_high = f > 0, f < fibres - 1

    weight_copies = [
        pltpu.make_async_copy(cw_hbm.at[0], cw.at[0], w_sem.at[0]),
        pltpu.make_async_copy(rw_hbm, rw, w_sem.at[1]),
        pltpu.make_async_copy(cw_hbm.at[1], cw.at[1], w_sem.at[2]),
        pltpu.make_async_copy(sw_hbm, sw, w_sem.at[3]),
        pltpu.make_async_copy(cb_hbm, cb_ref, w_sem.at[5]),
    ]
    for c in weight_copies:
        c.start()

    barrier = pltpu.get_barrier_semaphore()

    @pl.when(z > 0)
    def _():
        pl.semaphore_signal(barrier, inc=1, device_id={"tm": z - 1}, device_id_type=MESH)

    @pl.when(z < 3)
    def _():
        pl.semaphore_signal(barrier, inc=1, device_id={"tm": z + 1}, device_id_type=MESH)

    @pl.when(has_low)
    def _():
        pl.semaphore_signal(barrier, inc=1, device_id={"fibre": f - 1}, device_id_type=MESH)

    @pl.when(has_high)
    def _():
        pl.semaphore_signal(barrier, inc=1, device_id={"fibre": f + 1}, device_id_type=MESH)

    r_ids = lax.broadcasted_iota(jnp.int32, (rows, rows), 0)
    c_ids = lax.broadcasted_iota(jnp.int32, (rows, rows), 1)
    to_fibre_major = (
        (r_ids % HALF) * strips + r_ids // HALF == c_ids
    ).astype(jnp.float32).astype(jnp.bfloat16)

    x_copy.wait()
    for h in range(halves):
        chunk = x_ref[h * HALF:(h + 1) * HALF].reshape(rows, channels)
        turned = jnp.dot(to_fibre_major, chunk, preferred_element_type=jnp.float32)
        buf[M, h, 1:strips + 1] = turned.astype(jnp.bfloat16).reshape(strips, HALF, channels)

    edge_zero = jnp.zeros((1, HALF, channels), jnp.bfloat16)

    @pl.when(jnp.logical_not(has_low))
    def _():
        for k in (M, O, I, F, S1M, S1F):
            for h in range(halves):
                buf[k, h, 0:1] = edge_zero

    @pl.when(jnp.logical_not(has_high))
    def _():
        for k in (M, O, I, F, S1M, S1F):
            for h in range(halves):
                buf[k, h, strips + 1:strips + 2] = edge_zero

    pl.semaphore_wait(
        barrier,
        (z > 0).astype(jnp.int32) + (z < 3).astype(jnp.int32)
        + has_low.astype(jnp.int32) + has_high.astype(jnp.int32),
    )

    def spans(kind):
        edge = strips // 4 - (1 if kind == 3 else 0)
        return ((0, edge), (strips - edge, strips), (edge, strips - edge))

    def part_copy(src, dst, h, kind, to, part):
        low, high = spans(kind)[part]
        return pltpu.make_async_remote_copy(
            src_ref=buf.at[src, h, pl.ds(1 + low, high - low)],
            dst_ref=buf.at[dst, h, pl.ds(1 + low, high - low)],
            send_sem=send_sem.at[kind, h, part],
            recv_sem=recv_sem.at[dst, h, part],
            device_id={"tm": to},
            device_id_type=MESH,
        )

    def send(src, dst, h, kind, to, parts=(0, 1, 2)):
        for part in parts:
            part_copy(src, dst, h, kind, to, part).start()

    def drain(src, dst, h, kind, to):
        for part in range(3):
            part_copy(src, dst, h, kind, to, part).wait_send()

    def arrived(dst, h, parts, kind=0):
        for part in parts:
            part_copy(dst, dst, h, kind, inner, part).wait_recv()

    def halo_low(k, h):
        return pltpu.make_async_remote_copy(
            src_ref=buf.at[k, h, pl.ds(1, 1)],
            dst_ref=buf.at[k, h, pl.ds(strips + 1, 1)],
            send_sem=hsend.at[k, h, 0],
            recv_sem=hrecv.at[k, h, 0],
            device_id={"fibre": f - 1},
            device_id_type=MESH,
        )

    def halo_high(k, h):
        return pltpu.make_async_remote_copy(
            src_ref=buf.at[k, h, pl.ds(strips, 1)],
            dst_ref=buf.at[k, h, pl.ds(0, 1)],
            send_sem=hsend.at[k, h, 1],
            recv_sem=hrecv.at[k, h, 1],
            device_id={"fibre": f + 1},
            device_id_type=MESH,
        )

    def halo_start(k, h):
        @pl.when(has_low)
        def _():
            halo_low(k, h).start()

        @pl.when(has_high)
        def _():
            halo_high(k, h).start()

    def halo_wait(k, h):
        @pl.when(has_high)
        def _():
            halo_low(k, h).wait_recv()

        @pl.when(has_low)
        def _():
            halo_high(k, h).wait_recv()

    def halo_drain(k, h):
        @pl.when(has_low)
        def _():
            halo_low(k, h).wait_send()

        @pl.when(has_high)
        def _():
            halo_high(k, h).wait_send()

    def gate(layer, taps, h, low, high):
        total = cb_ref[layer:layer + 1]
        for k, tap in taps:
            views = [
                buf[k, h, b + low:b + high].reshape((high - low) * HALF, channels)
                for b in range(3)
            ]
            total = total + jnp.dot(
                jnp.concatenate(views, axis=1), cw[layer, tap],
                preferred_element_type=jnp.float32,
            )
        return (
            jnp.tanh(total[:, :channels]) * jax.nn.sigmoid(total[:, channels:])
        ).astype(jnp.bfloat16)

    def first_layer(dst, centre, taps, h, own=False, span=(0, strips)):
        low, high = span
        gated = gate(0, taps, h, low, high)
        base = buf[centre, h, 1 + low:1 + high].reshape(-1, channels).astype(jnp.float32)
        stream = base + jnp.dot(gated, rw[0], preferred_element_type=jnp.float32)
        buf[dst, h, 1 + low:1 + high] = stream.astype(jnp.bfloat16).reshape(
            high - low, HALF, channels
        )
        if own:
            skip[h] = jnp.dot(gated, sw[0], preferred_element_type=jnp.float32)

    def last_layer(h):
        gated = gate(1, ((S1M, 1), (S1F, tap_in)), h, 0, strips)
        base = buf[S1M, h, 1:strips + 1].reshape(rows, channels).astype(jnp.float32)
        stream = base + jnp.dot(gated, rw[1], preferred_element_type=jnp.float32)
        stream_ref[h] = stream.astype(jnp.bfloat16)
        total = skip[h] + jnp.dot(gated, sw[1], preferred_element_type=jnp.float32)
        rect_ref[h] = jnp.maximum(total, 0.0).astype(jnp.bfloat16)

    edges, middle = (0, 1), (2,)

    @pl.when(is_mid)
    def _():
        send(M, I, 0, 0, inner)
        send(M, I, 0, 1, outer)
        for h in range(halves):
            halo_start(M, h)
        send(M, I, 1, 1, outer)
        for part in range(3):
            arrived(O, 0, (part,))
            send(O, F, 0, 2, inner, (part,))
            if part == 1:
                halo_start(O, 0)
        send(M, I, 1, 0, inner)
        arrived(I, 0, edges)
        halo_start(I, 0)
        arrived(I, 0, middle)
        halo_wait(M, 0)
        halo_wait(O, 0)
        halo_wait(I, 0)
        for c in (0, 1, 3, 4):
            weight_copies[c].wait()
        own_taps = ((O, tap_out), (M, 1), (I, tap_in))
        inner_taps = ((M, tap_out), (I, 1), (F, tap_in))
        far_taps = ((I, tap_out), (F, 1))
        first_layer(S1M, M, own_taps, 0, own=True)
        halo_start(S1M, 0)
        for part in range(3):
            arrived(O, 1, (part,))
            send(O, F, 1, 2, inner, (part,))
        halo_start(O, 1)

        def far_blocks(h):
            arrived(F, h, edges)
            halo_start(F, h)
            halo_wait(F, h)
            for part in edges:
                first_layer(S1I, I, inner_taps, h, span=spans(3)[part])
            send(S1I, S1F, h, 3, outer, edges)
            arrived(F, h, middle)
            first_layer(S1I, I, inner_taps, h, span=spans(3)[2])
            send(S1I, S1F, h, 3, outer, middle)
            first_layer(S1F, F, far_taps, h)
            halo_start(S1F, h)

        far_blocks(0)
        arrived(I, 1, edges)
        halo_start(I, 1)
        arrived(I, 1, middle)
        halo_wait(M, 1)
        halo_wait(O, 1)
        halo_wait(I, 1)
        first_layer(S1M, M, own_taps, 1, own=True)
        halo_start(S1M, 1)
        halo_wait(S1M, 0)
        halo_wait(S1F, 0)
        weight_copies[2].wait()
        last_layer(0)
        far_blocks(1)
        halo_wait(S1M, 1)
        halo_wait(S1F, 1)
        last_layer(1)
        for h in range(halves):
            drain(M, I, h, 0, inner)
            drain(M, I, h, 1, outer)
            drain(O, F, h, 2, inner)
            drain(S1I, S1F, h, 3, outer)
            for k in (O, F):
                halo_drain(k, h)

    @pl.when(is_end)
    def _():
        for h in range(halves):
            send(M, O, h, 0, inner)
        for h in range(halves):
            halo_start(M, h)
        for c in (0, 1, 3, 4):
            weight_copies[c].wait()
        for h in range(halves):
            arrived(I, h, edges)
            halo_start(I, h)
            arrived(I, h, middle)
            halo_wait(M, h)
            halo_wait(I, h)
            first_layer(S1M, M, ((M, 1), (I, tap_in)), h, own=True)
            halo_start(S1M, h)
        weight_copies[2].wait()
        for h in range(halves):
            arrived(S1F, h, edges, 3)
            halo_start(S1F, h)
            arrived(S1F, h, middle, 3)
            halo_wait(S1M, h)
            halo_wait(S1F, h)
            last_layer(h)
        for h in range(halves):
            drain(M, O, h, 0, inner)

    for h in range(halves):
        for k in (M, I, S1M, S1F):
            halo_drain(k, h)


def head_kernel(stream_ref, rect_ref, hd_ref, res_ref, out_ref):
    times, strips, channels = res_ref.shape
    rows = times * strips
    r_ids = lax.broadcasted_iota(jnp.int32, (rows, rows), 0)
    c_ids = lax.broadcasted_iota(jnp.int32, (rows, rows), 1)
    to_time_major = (
        (c_ids % HALF) * strips + c_ids // HALF == r_ids
    ).astype(jnp.float32).astype(jnp.bfloat16)

    def turned(block):
        return jnp.dot(
            to_time_major, block, preferred_element_type=jnp.float32
        ).astype(jnp.bfloat16)

    res_ref[...] = turned(stream_ref[0]).reshape(times, strips, channels)
    out_ref[...] = jnp.dot(
        turned(rect_ref[0]), hd_ref[...], preferred_element_type=jnp.float32
    ).astype(jnp.bfloat16).reshape(times, strips, -1)


def fused(recording, conv_weight, conv_bias, res_weight, skip_weight, head_weight):
    times, strips, channels = recording.shape
    layers = conv_weight.shape[0]
    halves = times // HALF
    rows = HALF * strips
    pixels = head_weight.shape[1]
    vmem = pl.BlockSpec(memory_space=pltpu.VMEM)
    hbm = pl.BlockSpec(memory_space=pl.ANY)
    weights = conv_weight.reshape(layers, 3, 3 * channels, 2 * channels)
    flat = jax.ShapeDtypeStruct((halves, rows, channels), jnp.bfloat16)
    stream, rectified = pl.pallas_call(
        fused_kernel,
        out_shape=(flat, flat),
        in_specs=[hbm] * 5,
        out_specs=(vmem, vmem),
        scratch_shapes=[
            pltpu.VMEM(recording.shape, jnp.bfloat16),
            pltpu.VMEM(conv_bias.shape, jnp.float32),
            pltpu.VMEM((7, halves, strips + 2, HALF, channels), jnp.bfloat16),
            pltpu.VMEM(weights.shape, jnp.bfloat16),
            pltpu.VMEM(res_weight.shape, jnp.bfloat16),
            pltpu.VMEM(skip_weight.shape, jnp.bfloat16),
            pltpu.VMEM((halves, rows, channels), jnp.float32),
            pltpu.SemaphoreType.DMA((6,)),
            pltpu.SemaphoreType.DMA((4, halves, 3)),
            pltpu.SemaphoreType.DMA((7, halves, 3)),
            pltpu.SemaphoreType.DMA((7, halves, 2)),
            pltpu.SemaphoreType.DMA((7, halves, 2)),
        ],
        compiler_params=pltpu.CompilerParams(
            collective_id=0, has_side_effects=True, vmem_limit_bytes=62 * 2**20
        ),
        cost_estimate=pl.CostEstimate(
            flops=10**10, bytes_accessed=10**7, transcendentals=10**6
        ),
    )(recording, weights, conv_bias, res_weight, skip_weight)
    block = pl.BlockSpec((1, rows, channels), lambda h: (h, 0, 0))
    return pl.pallas_call(
        head_kernel,
        grid=(halves,),
        out_shape=(
            jax.ShapeDtypeStruct((times, strips, channels), jnp.bfloat16),
            jax.ShapeDtypeStruct((times, strips, pixels), jnp.bfloat16),
        ),
        in_specs=[block, block, pl.BlockSpec((channels, pixels), lambda h: (0, 0))],
        out_specs=(
            pl.BlockSpec((HALF, strips, channels), lambda h: (h, 0, 0)),
            pl.BlockSpec((HALF, strips, pixels), lambda h: (h, 0, 0)),
        ),
        compiler_params=pltpu.CompilerParams(vmem_limit_bytes=62 * 2**20),
        cost_estimate=pl.CostEstimate(
            flops=10**9, bytes_accessed=4 * 10**6, transcendentals=0
        ),
    )(stream, rectified, head_weight)


def program(recording, conv_weight, *rest):
    four = lax.axis_size("tm") == 4
    if four and recording.shape[0] == DILATION_SPAN and conv_weight.shape[0] == 2:
        return fused(recording, conv_weight, *rest)
    return local(recording, conv_weight, *rest)


def solution(mesh):
    return jax.shard_map(
        program,
        mesh=mesh,
        in_specs=(P(("groups", "tm"), "fibre", None), P(), P(), P(), P(), P()),
        out_specs=(P(("groups", "tm"), "fibre", None), P(("groups", "tm"), "fibre", None)),
        check_vma=False,
    )
```

```python
import jax
import jax.numpy as jnp
from jax import lax
from jax.experimental import pallas as pl
from jax.experimental.pallas import tpu as pltpu
from jax.sharding import PartitionSpec as P

DILATION_SPAN = 32


def passed_along(shard, axis, by):
    devices = lax.axis_size(axis)
    pairs = [(i, i + by) for i in range(devices) if 0 <= i + by < devices]
    return lax.ppermute(shard, axis, pairs)


def padded(block, sides, width):
    for axis, dim in sides:
        count = lax.axis_size(axis)
        forward = [(i, i + 1) for i in range(count - 1)]
        backward = [(target, source) for source, target in forward]
        low = lax.ppermute(
            lax.slice_in_dim(block, block.shape[dim] - width, None, axis=dim), axis, forward
        )
        high = lax.ppermute(lax.slice_in_dim(block, 0, width, axis=dim), axis, backward)
        block = jnp.concatenate([low, block, high], axis=dim)
    return block


def gate_layer(earlier, middle, later, layer_weight, layer_bias):
    channels = middle.shape[-1]
    fibre_rows = middle.shape[-2] - 2
    summed = None
    for time_offset, block in enumerate((earlier, middle, later)):
        for fibre_offset in range(3):
            receptive_view = block[..., fibre_offset : fibre_offset + fibre_rows, :].reshape(
                -1, channels
            )
            product = jnp.dot(
                receptive_view,
                layer_weight[time_offset, fibre_offset],
                preferred_element_type=jnp.float32,
            )
            summed = product if summed is None else summed + product
    before_gate = summed + layer_bias
    return (jnp.tanh(before_gate[:, :channels]) * jax.nn.sigmoid(before_gate[:, channels:])).astype(
        jnp.bfloat16
    )


def update(gated, stream_rows, skipped, layer_res, layer_skip):
    new_stream = (
        stream_rows.astype(jnp.float32)
        + jnp.dot(gated, layer_res, preferred_element_type=jnp.float32)
    ).astype(jnp.bfloat16)
    new_skip = skipped + jnp.dot(gated, layer_skip, preferred_element_type=jnp.float32)
    return (new_stream, new_skip)


def head_out(skipped, head_weight):
    rectified = jnp.maximum(skipped, 0.0).astype(jnp.bfloat16)
    return jnp.dot(rectified, head_weight, preferred_element_type=jnp.float32).astype(jnp.bfloat16)


def local(recording, conv_weight, conv_bias, res_weight, skip_weight, head_weight):
    time_slices, strips, channels = recording.shape
    layer_count = conv_weight.shape[0]
    stream = recording
    skipped = jnp.zeros((time_slices * strips, channels), jnp.float32)
    for layer in range(layer_count):
        tap_spacing = DILATION_SPAN * 2**layer // time_slices
        earlier_bare = passed_along(stream, "tm", tap_spacing)
        later_bare = passed_along(stream, "tm", -tap_spacing)
        stacked = jnp.stack([earlier_bare, stream, later_bare])
        border_filled = padded(stacked, (("fibre", 2),), 1)
        earlier, middle, later = (border_filled[0], border_filled[1], border_filled[2])
        gated = gate_layer(earlier, middle, later, conv_weight[layer], conv_bias[layer])
        new_rows, skipped = update(
            gated, stream.reshape(-1, channels), skipped, res_weight[layer], skip_weight[layer]
        )
        stream = new_rows.reshape(time_slices, strips, channels)
    denoised = head_out(skipped, head_weight)
    return (stream, denoised.reshape(time_slices, strips, -1))


MESH = pl.DeviceIdType.MESH
M, O, I, F, S1M, S1F, S1I = range(7)
HALF = 16


def fused_kernel(x_hbm, cw_hbm, cb_hbm, rw_hbm, sw_hbm, stream_ref, rect_ref,
                 x_ref, cb_ref, buf, cw, rw, sw, skip, partial, w_sem, send_sem, recv_sem, hsend, hrecv):
    x_copy = pltpu.make_async_copy(x_hbm, x_ref, w_sem.at[4])
    x_copy.start()
    strips = x_ref.shape[1]
    channels = x_ref.shape[2]
    halves = x_ref.shape[0] // HALF
    rows = HALF * strips
    z = lax.axis_index("tm")
    f = lax.axis_index("fibre")
    fibres = lax.axis_size("fibre")
    is_mid = jnp.logical_or(z == 1, z == 2)
    is_end = jnp.logical_not(is_mid)
    toward = jnp.where(z < 2, 1, -1)
    inner = z + toward
    outer = jnp.clip(z - toward, 0, 3)
    tap_in = 1 + toward
    tap_out = 1 - toward
    has_low, has_high = f > 0, f < fibres - 1

    weight_copies = [
        pltpu.make_async_copy(cw_hbm.at[0], cw.at[0], w_sem.at[0]),
        pltpu.make_async_copy(rw_hbm, rw, w_sem.at[1]),
        pltpu.make_async_copy(cw_hbm.at[1], cw.at[1], w_sem.at[2]),
        pltpu.make_async_copy(sw_hbm, sw, w_sem.at[3]),
        pltpu.make_async_copy(cb_hbm, cb_ref, w_sem.at[5]),
    ]
    for c in weight_copies:
        c.start()

    barrier = pltpu.get_barrier_semaphore()

    @pl.when(z > 0)
    def _():
        pl.semaphore_signal(barrier, inc=1, device_id={"tm": z - 1}, device_id_type=MESH)

    @pl.when(z < 3)
    def _():
        pl.semaphore_signal(barrier, inc=1, device_id={"tm": z + 1}, device_id_type=MESH)

    @pl.when(has_low)
    def _():
        pl.semaphore_signal(barrier, inc=1, device_id={"fibre": f - 1}, device_id_type=MESH)

    @pl.when(has_high)
    def _():
        pl.semaphore_signal(barrier, inc=1, device_id={"fibre": f + 1}, device_id_type=MESH)

    r_ids = lax.broadcasted_iota(jnp.int32, (rows, rows), 0)
    c_ids = lax.broadcasted_iota(jnp.int32, (rows, rows), 1)
    to_fibre_major = (
        (r_ids % HALF) * strips + r_ids // HALF == c_ids
    ).astype(jnp.float32).astype(jnp.bfloat16)

    x_copy.wait()
    for h in range(halves):
        chunk = x_ref[h * HALF:(h + 1) * HALF].reshape(rows, channels)
        turned = jnp.dot(to_fibre_major, chunk, preferred_element_type=jnp.float32)
        buf[M, h, 1:strips + 1] = turned.astype(jnp.bfloat16).reshape(strips, HALF, channels)

    edge_zero = jnp.zeros((1, HALF, channels), jnp.bfloat16)

    @pl.when(jnp.logical_not(has_low))
    def _():
        for k in (M, O, I, F, S1M, S1F):
            for h in range(halves):
                buf[k, h, 0:1] = edge_zero

    @pl.when(jnp.logical_not(has_high))
    def _():
        for k in (M, O, I, F, S1M, S1F):
            for h in range(halves):
                buf[k, h, strips + 1:strips + 2] = edge_zero

    pl.semaphore_wait(
        barrier,
        (z > 0).astype(jnp.int32) + (z < 3).astype(jnp.int32)
        + has_low.astype(jnp.int32) + has_high.astype(jnp.int32),
    )

    def spans(kind):
        edge = strips // 4 - (1 if kind == 3 else 0)
        return ((0, edge), (strips - edge, strips), (edge, strips - edge))

    def part_copy(src, dst, h, kind, to, part):
        low, high = spans(kind)[part]
        return pltpu.make_async_remote_copy(
            src_ref=buf.at[src, h, pl.ds(1 + low, high - low)],
            dst_ref=buf.at[dst, h, pl.ds(1 + low, high - low)],
            send_sem=send_sem.at[kind, h, part],
            recv_sem=recv_sem.at[dst, h, part],
            device_id={"tm": to},
            device_id_type=MESH,
        )

    def send(src, dst, h, kind, to, parts=(0, 1, 2)):
        for part in parts:
            part_copy(src, dst, h, kind, to, part).start()

    def drain(src, dst, h, kind, to):
        for part in range(3):
            part_copy(src, dst, h, kind, to, part).wait_send()

    def arrived(dst, h, parts, kind=0):
        for part in parts:
            part_copy(dst, dst, h, kind, inner, part).wait_recv()

    def halo_low(k, h):
        return pltpu.make_async_remote_copy(
            src_ref=buf.at[k, h, pl.ds(1, 1)],
            dst_ref=buf.at[k, h, pl.ds(strips + 1, 1)],
            send_sem=hsend.at[k, h, 0],
            recv_sem=hrecv.at[k, h, 0],
            device_id={"fibre": f - 1},
            device_id_type=MESH,
        )

    def halo_high(k, h):
        return pltpu.make_async_remote_copy(
            src_ref=buf.at[k, h, pl.ds(strips, 1)],
            dst_ref=buf.at[k, h, pl.ds(0, 1)],
            send_sem=hsend.at[k, h, 1],
            recv_sem=hrecv.at[k, h, 1],
            device_id={"fibre": f + 1},
            device_id_type=MESH,
        )

    def halo_start(k, h):
        @pl.when(has_low)
        def _():
            halo_low(k, h).start()

        @pl.when(has_high)
        def _():
            halo_high(k, h).start()

    def halo_wait(k, h):
        @pl.when(has_high)
        def _():
            halo_low(k, h).wait_recv()

        @pl.when(has_low)
        def _():
            halo_high(k, h).wait_recv()

    def halo_drain(k, h):
        @pl.when(has_low)
        def _():
            halo_low(k, h).wait_send()

        @pl.when(has_high)
        def _():
            halo_high(k, h).wait_send()

    def added(total, layer, taps, h, low, high):
        for k, tap in taps:
            views = [
                buf[k, h, b + low:b + high].reshape((high - low) * HALF, channels)
                for b in range(3)
            ]
            total = total + jnp.dot(
                jnp.concatenate(views, axis=1), cw[layer, tap],
                preferred_element_type=jnp.float32,
            )
        return total

    def prepare(slot, layer, taps, h):
        partial[slot] = added(cb_ref[layer:layer + 1], layer, taps, h, 0, strips)

    def gate(layer, taps, h, low, high, slot=None):
        if slot is None:
            total = cb_ref[layer:layer + 1]
        else:
            total = partial[slot, low * HALF:high * HALF]
        total = added(total, layer, taps, h, low, high)
        return (
            jnp.tanh(total[:, :channels]) * jax.nn.sigmoid(total[:, channels:])
        ).astype(jnp.bfloat16)

    def first_layer(dst, centre, taps, h, own=False, span=(0, strips), slot=None):
        low, high = span
        gated = gate(0, taps, h, low, high, slot)
        base = buf[centre, h, 1 + low:1 + high].reshape(-1, channels).astype(jnp.float32)
        stream = base + jnp.dot(gated, rw[0], preferred_element_type=jnp.float32)
        buf[dst, h, 1 + low:1 + high] = stream.astype(jnp.bfloat16).reshape(
            high - low, HALF, channels
        )
        if own:
            skip[h] = jnp.dot(gated, sw[0], preferred_element_type=jnp.float32)

    def last_layer(h):
        gated = gate(1, ((S1F, tap_in),), h, 0, strips, 2)
        base = buf[S1M, h, 1:strips + 1].reshape(rows, channels).astype(jnp.float32)
        stream = base + jnp.dot(gated, rw[1], preferred_element_type=jnp.float32)
        stream_ref[h] = stream.astype(jnp.bfloat16)
        total = skip[h] + jnp.dot(gated, sw[1], preferred_element_type=jnp.float32)
        rect_ref[h] = jnp.maximum(total, 0.0).astype(jnp.bfloat16)

    edges, middle = (0, 1), (2,)

    @pl.when(is_mid)
    def _():
        send(M, I, 0, 0, inner)
        send(M, I, 0, 1, outer)
        for h in range(halves):
            halo_start(M, h)
        send(M, I, 1, 1, outer)
        for part in range(3):
            arrived(O, 0, (part,))
            send(O, F, 0, 2, inner, (part,))
            if part == 1:
                halo_start(O, 0)
        send(M, I, 1, 0, inner)
        arrived(I, 0, edges)
        halo_start(I, 0)
        arrived(I, 0, middle)
        halo_wait(M, 0)
        halo_wait(O, 0)
        halo_wait(I, 0)
        for c in (0, 1, 3, 4):
            weight_copies[c].wait()
        own_taps = ((O, tap_out), (M, 1), (I, tap_in))
        inner_taps = ((F, tap_in),)
        far_taps = ((F, 1),)
        first_layer(S1M, M, own_taps, 0, own=True)
        halo_start(S1M, 0)
        for part in range(3):
            arrived(O, 1, (part,))
            send(O, F, 1, 2, inner, (part,))
        halo_start(O, 1)

        def far_blocks(h):
            prepare(0, 0, ((M, tap_out), (I, 1)), h)
            prepare(1, 0, ((I, tap_out),), h)
            arrived(F, h, edges)
            halo_start(F, h)
            halo_wait(F, h)
            for part in edges:
                first_layer(S1I, I, inner_taps, h, span=spans(3)[part], slot=0)
            send(S1I, S1F, h, 3, outer, edges)
            arrived(F, h, middle)
            first_layer(S1I, I, inner_taps, h, span=spans(3)[2], slot=0)
            send(S1I, S1F, h, 3, outer, middle)
            first_layer(S1F, F, far_taps, h, slot=1)
            halo_start(S1F, h)

        far_blocks(0)
        arrived(I, 1, edges)
        halo_start(I, 1)
        arrived(I, 1, middle)
        halo_wait(M, 1)
        halo_wait(O, 1)
        halo_wait(I, 1)
        first_layer(S1M, M, own_taps, 1, own=True)
        halo_start(S1M, 1)
        halo_wait(S1M, 0)
        halo_wait(S1F, 0)
        weight_copies[2].wait()
        prepare(2, 1, ((S1M, 1),), 0)
        last_layer(0)
        halo_wait(S1M, 1)
        prepare(2, 1, ((S1M, 1),), 1)
        far_blocks(1)
        halo_wait(S1F, 1)
        last_layer(1)
        for h in range(halves):
            drain(M, I, h, 0, inner)
            drain(M, I, h, 1, outer)
            drain(O, F, h, 2, inner)
            drain(S1I, S1F, h, 3, outer)
            for k in (O, F):
                halo_drain(k, h)

    @pl.when(is_end)
    def _():
        for h in range(halves):
            send(M, O, h, 0, inner)
        for h in range(halves):
            halo_start(M, h)
        for c in (0, 1, 3, 4):
            weight_copies[c].wait()
        for h in range(halves):
            arrived(I, h, edges)
            halo_start(I, h)
            arrived(I, h, middle)
            halo_wait(M, h)
            halo_wait(I, h)
            first_layer(S1M, M, ((M, 1), (I, tap_in)), h, own=True)
            halo_start(S1M, h)
        weight_copies[2].wait()
        for h in range(halves):
            halo_wait(S1M, h)
            prepare(2, 1, ((S1M, 1),), h)
            arrived(S1F, h, edges, 3)
            halo_start(S1F, h)
            arrived(S1F, h, middle, 3)
            halo_wait(S1F, h)
            last_layer(h)
        for h in range(halves):
            drain(M, O, h, 0, inner)

    for h in range(halves):
        for k in (M, I, S1M, S1F):
            halo_drain(k, h)


def head_kernel(stream_ref, rect_ref, hd_ref, res_ref, out_ref):
    times, strips, channels = res_ref.shape
    rows = times * strips
    r_ids = lax.broadcasted_iota(jnp.int32, (rows, rows), 0)
    c_ids = lax.broadcasted_iota(jnp.int32, (rows, rows), 1)
    to_time_major = (
        (c_ids % HALF) * strips + c_ids // HALF == r_ids
    ).astype(jnp.float32).astype(jnp.bfloat16)

    def turned(block):
        return jnp.dot(
            to_time_major, block, preferred_element_type=jnp.float32
        ).astype(jnp.bfloat16)

    res_ref[...] = turned(stream_ref[0]).reshape(times, strips, channels)
    out_ref[...] = jnp.dot(
        turned(rect_ref[0]), hd_ref[...], preferred_element_type=jnp.float32
    ).astype(jnp.bfloat16).reshape(times, strips, -1)


def fused(recording, conv_weight, conv_bias, res_weight, skip_weight, head_weight):
    times, strips, channels = recording.shape
    layers = conv_weight.shape[0]
    halves = times // HALF
    rows = HALF * strips
    pixels = head_weight.shape[1]
    vmem = pl.BlockSpec(memory_space=pltpu.VMEM)
    hbm = pl.BlockSpec(memory_space=pl.ANY)
    weights = conv_weight.reshape(layers, 3, 3 * channels, 2 * channels)
    flat = jax.ShapeDtypeStruct((halves, rows, channels), jnp.bfloat16)
    stream, rectified = pl.pallas_call(
        fused_kernel,
        out_shape=(flat, flat),
        in_specs=[hbm] * 5,
        out_specs=(vmem, vmem),
        scratch_shapes=[
            pltpu.VMEM(recording.shape, jnp.bfloat16),
            pltpu.VMEM(conv_bias.shape, jnp.float32),
            pltpu.VMEM((7, halves, strips + 2, HALF, channels), jnp.bfloat16),
            pltpu.VMEM(weights.shape, jnp.bfloat16),
            pltpu.VMEM(res_weight.shape, jnp.bfloat16),
            pltpu.VMEM(skip_weight.shape, jnp.bfloat16),
            pltpu.VMEM((halves, rows, channels), jnp.float32),
            pltpu.VMEM((3, rows, 2 * channels), jnp.float32),
            pltpu.SemaphoreType.DMA((6,)),
            pltpu.SemaphoreType.DMA((4, halves, 3)),
            pltpu.SemaphoreType.DMA((7, halves, 3)),
            pltpu.SemaphoreType.DMA((7, halves, 2)),
            pltpu.SemaphoreType.DMA((7, halves, 2)),
        ],
        compiler_params=pltpu.CompilerParams(
            collective_id=0, has_side_effects=True, vmem_limit_bytes=62 * 2**20
        ),
        cost_estimate=pl.CostEstimate(
            flops=10**10, bytes_accessed=10**7, transcendentals=10**6
        ),
    )(recording, weights, conv_bias, res_weight, skip_weight)
    block = pl.BlockSpec((1, rows, channels), lambda h: (h, 0, 0))
    return pl.pallas_call(
        head_kernel,
        grid=(halves,),
        out_shape=(
            jax.ShapeDtypeStruct((times, strips, channels), jnp.bfloat16),
            jax.ShapeDtypeStruct((times, strips, pixels), jnp.bfloat16),
        ),
        in_specs=[block, block, pl.BlockSpec((channels, pixels), lambda h: (0, 0))],
        out_specs=(
            pl.BlockSpec((HALF, strips, channels), lambda h: (h, 0, 0)),
            pl.BlockSpec((HALF, strips, pixels), lambda h: (h, 0, 0)),
        ),
        compiler_params=pltpu.CompilerParams(vmem_limit_bytes=62 * 2**20),
        cost_estimate=pl.CostEstimate(
            flops=10**9, bytes_accessed=4 * 10**6, transcendentals=0
        ),
    )(stream, rectified, head_weight)


def program(recording, conv_weight, *rest):
    four = lax.axis_size("tm") == 4
    if four and recording.shape[0] == DILATION_SPAN and conv_weight.shape[0] == 2:
        return fused(recording, conv_weight, *rest)
    return local(recording, conv_weight, *rest)


def solution(mesh):
    return jax.shard_map(
        program,
        mesh=mesh,
        in_specs=(P(("groups", "tm"), "fibre", None), P(), P(), P(), P(), P()),
        out_specs=(P(("groups", "tm"), "fibre", None), P(("groups", "tm"), "fibre", None)),
        check_vma=False,
    )
```

```python
import jax
import jax.numpy as jnp
from jax import lax
from jax.experimental import pallas as pl
from jax.experimental.pallas import tpu as pltpu
from jax.sharding import PartitionSpec as P

DILATION_SPAN = 32


def passed_along(shard, axis, by):
    devices = lax.axis_size(axis)
    pairs = [(i, i + by) for i in range(devices) if 0 <= i + by < devices]
    return lax.ppermute(shard, axis, pairs)


def padded(block, sides, width):
    for axis, dim in sides:
        count = lax.axis_size(axis)
        forward = [(i, i + 1) for i in range(count - 1)]
        backward = [(target, source) for source, target in forward]
        low = lax.ppermute(
            lax.slice_in_dim(block, block.shape[dim] - width, None, axis=dim), axis, forward
        )
        high = lax.ppermute(lax.slice_in_dim(block, 0, width, axis=dim), axis, backward)
        block = jnp.concatenate([low, block, high], axis=dim)
    return block


def gate_layer(earlier, middle, later, layer_weight, layer_bias):
    channels = middle.shape[-1]
    fibre_rows = middle.shape[-2] - 2
    summed = None
    for time_offset, block in enumerate((earlier, middle, later)):
        for fibre_offset in range(3):
            receptive_view = block[..., fibre_offset : fibre_offset + fibre_rows, :].reshape(
                -1, channels
            )
            product = jnp.dot(
                receptive_view,
                layer_weight[time_offset, fibre_offset],
                preferred_element_type=jnp.float32,
            )
            summed = product if summed is None else summed + product
    before_gate = summed + layer_bias
    return (jnp.tanh(before_gate[:, :channels]) * jax.nn.sigmoid(before_gate[:, channels:])).astype(
        jnp.bfloat16
    )


def update(gated, stream_rows, skipped, layer_res, layer_skip):
    new_stream = (
        stream_rows.astype(jnp.float32)
        + jnp.dot(gated, layer_res, preferred_element_type=jnp.float32)
    ).astype(jnp.bfloat16)
    new_skip = skipped + jnp.dot(gated, layer_skip, preferred_element_type=jnp.float32)
    return (new_stream, new_skip)


def head_out(skipped, head_weight):
    rectified = jnp.maximum(skipped, 0.0).astype(jnp.bfloat16)
    return jnp.dot(rectified, head_weight, preferred_element_type=jnp.float32).astype(jnp.bfloat16)


def local(recording, conv_weight, conv_bias, res_weight, skip_weight, head_weight):
    time_slices, strips, channels = recording.shape
    layer_count = conv_weight.shape[0]
    stream = recording
    skipped = jnp.zeros((time_slices * strips, channels), jnp.float32)
    for layer in range(layer_count):
        tap_spacing = DILATION_SPAN * 2**layer // time_slices
        earlier_bare = passed_along(stream, "tm", tap_spacing)
        later_bare = passed_along(stream, "tm", -tap_spacing)
        stacked = jnp.stack([earlier_bare, stream, later_bare])
        border_filled = padded(stacked, (("fibre", 2),), 1)
        earlier, middle, later = (border_filled[0], border_filled[1], border_filled[2])
        gated = gate_layer(earlier, middle, later, conv_weight[layer], conv_bias[layer])
        new_rows, skipped = update(
            gated, stream.reshape(-1, channels), skipped, res_weight[layer], skip_weight[layer]
        )
        stream = new_rows.reshape(time_slices, strips, channels)
    denoised = head_out(skipped, head_weight)
    return (stream, denoised.reshape(time_slices, strips, -1))


MESH = pl.DeviceIdType.MESH
M, O, I, F, S1M, S1F, S1I = range(7)
HALF = 16


def fused_kernel(x_hbm, cw_hbm, cb_hbm, rw_hbm, sw_hbm, stream_ref, rect_ref,
                 x_ref, cb_ref, buf, cw, rw, sw, skip, x_sem, w_sem, send_sem, recv_sem, hsend, hrecv):
    x_copies = [
        pltpu.make_async_copy(
            x_hbm.at[pl.ds(h * HALF, HALF)], x_ref.at[pl.ds(h * HALF, HALF)], x_sem.at[h]
        )
        for h in range(x_ref.shape[0] // HALF)
    ]
    for c in x_copies:
        c.start()
    strips = x_ref.shape[1]
    channels = x_ref.shape[2]
    halves = x_ref.shape[0] // HALF
    rows = HALF * strips
    z = lax.axis_index("tm")
    f = lax.axis_index("fibre")
    fibres = lax.axis_size("fibre")
    is_mid = jnp.logical_or(z == 1, z == 2)
    is_end = jnp.logical_not(is_mid)
    toward = jnp.where(z < 2, 1, -1)
    inner = z + toward
    outer = jnp.clip(z - toward, 0, 3)
    tap_in = 1 + toward
    tap_out = 1 - toward
    has_low, has_high = f > 0, f < fibres - 1

    weight_copies = [
        pltpu.make_async_copy(cw_hbm.at[0], cw.at[0], w_sem.at[0]),
        pltpu.make_async_copy(rw_hbm, rw, w_sem.at[1]),
        pltpu.make_async_copy(cw_hbm.at[1], cw.at[1], w_sem.at[2]),
        pltpu.make_async_copy(sw_hbm, sw, w_sem.at[3]),
        pltpu.make_async_copy(cb_hbm, cb_ref, w_sem.at[5]),
    ]
    for c in weight_copies:
        c.start()

    barrier = pltpu.get_barrier_semaphore()

    @pl.when(z > 0)
    def _():
        pl.semaphore_signal(barrier, inc=1, device_id={"tm": z - 1}, device_id_type=MESH)

    @pl.when(z < 3)
    def _():
        pl.semaphore_signal(barrier, inc=1, device_id={"tm": z + 1}, device_id_type=MESH)

    @pl.when(has_low)
    def _():
        pl.semaphore_signal(barrier, inc=1, device_id={"fibre": f - 1}, device_id_type=MESH)

    @pl.when(has_high)
    def _():
        pl.semaphore_signal(barrier, inc=1, device_id={"fibre": f + 1}, device_id_type=MESH)

    r_ids = lax.broadcasted_iota(jnp.int32, (rows, rows), 0)
    c_ids = lax.broadcasted_iota(jnp.int32, (1, rows), 1)
    to_fibre_major = (
        (c_ids % strips) * HALF + c_ids // strips == r_ids
    ).astype(jnp.float32).astype(jnp.bfloat16)

    def turn(h):
        x_copies[h].wait()
        chunk = x_ref[h * HALF:(h + 1) * HALF].reshape(rows, channels)
        turned = jnp.dot(to_fibre_major, chunk, preferred_element_type=jnp.float32)
        buf[M, h, 1:strips + 1] = turned.astype(jnp.bfloat16).reshape(strips, HALF, channels)

    turn(0)

    edge_zero = jnp.zeros((1, HALF, channels), jnp.bfloat16)

    @pl.when(jnp.logical_not(has_low))
    def _():
        for k in (M, O, I, F, S1M, S1F):
            for h in range(halves):
                buf[k, h, 0:1] = edge_zero

    @pl.when(jnp.logical_not(has_high))
    def _():
        for k in (M, O, I, F, S1M, S1F):
            for h in range(halves):
                buf[k, h, strips + 1:strips + 2] = edge_zero

    pl.semaphore_wait(
        barrier,
        (z > 0).astype(jnp.int32) + (z < 3).astype(jnp.int32)
        + has_low.astype(jnp.int32) + has_high.astype(jnp.int32),
    )

    def spans(kind):
        edge = strips // 4 - (1 if kind == 3 else 0)
        return ((0, edge), (strips - edge, strips), (edge, strips - edge))

    def part_copy(src, dst, h, kind, to, part):
        low, high = spans(kind)[part]
        return pltpu.make_async_remote_copy(
            src_ref=buf.at[src, h, pl.ds(1 + low, high - low)],
            dst_ref=buf.at[dst, h, pl.ds(1 + low, high - low)],
            send_sem=send_sem.at[kind, h, part],
            recv_sem=recv_sem.at[dst, h, part],
            device_id={"tm": to},
            device_id_type=MESH,
        )

    def send(src, dst, h, kind, to, parts=(0, 1, 2)):
        for part in parts:
            part_copy(src, dst, h, kind, to, part).start()

    def drain(src, dst, h, kind, to):
        for part in range(3):
            part_copy(src, dst, h, kind, to, part).wait_send()

    def arrived(dst, h, parts, kind=0):
        for part in parts:
            part_copy(dst, dst, h, kind, inner, part).wait_recv()

    def halo_low(k, h):
        return pltpu.make_async_remote_copy(
            src_ref=buf.at[k, h, pl.ds(1, 1)],
            dst_ref=buf.at[k, h, pl.ds(strips + 1, 1)],
            send_sem=hsend.at[k, h, 0],
            recv_sem=hrecv.at[k, h, 0],
            device_id={"fibre": f - 1},
            device_id_type=MESH,
        )

    def halo_high(k, h):
        return pltpu.make_async_remote_copy(
            src_ref=buf.at[k, h, pl.ds(strips, 1)],
            dst_ref=buf.at[k, h, pl.ds(0, 1)],
            send_sem=hsend.at[k, h, 1],
            recv_sem=hrecv.at[k, h, 1],
            device_id={"fibre": f + 1},
            device_id_type=MESH,
        )

    def halo_start(k, h):
        @pl.when(has_low)
        def _():
            halo_low(k, h).start()

        @pl.when(has_high)
        def _():
            halo_high(k, h).start()

    def halo_wait(k, h):
        @pl.when(has_high)
        def _():
            halo_low(k, h).wait_recv()

        @pl.when(has_low)
        def _():
            halo_high(k, h).wait_recv()

    def halo_drain(k, h):
        @pl.when(has_low)
        def _():
            halo_low(k, h).wait_send()

        @pl.when(has_high)
        def _():
            halo_high(k, h).wait_send()

    def gate(layer, taps, h, low, high):
        total = cb_ref[layer:layer + 1]
        for k, tap in taps:
            views = [
                buf[k, h, b + low:b + high].reshape((high - low) * HALF, channels)
                for b in range(3)
            ]
            total = total + jnp.dot(
                jnp.concatenate(views, axis=1), cw[layer, tap],
                preferred_element_type=jnp.float32,
            )
        return (
            jnp.tanh(total[:, :channels]) * jax.nn.sigmoid(total[:, channels:])
        ).astype(jnp.bfloat16)

    def first_layer(dst, centre, taps, h, own=False, span=(0, strips)):
        low, high = span
        gated = gate(0, taps, h, low, high)
        base = buf[centre, h, 1 + low:1 + high].reshape(-1, channels).astype(jnp.float32)
        stream = base + jnp.dot(gated, rw[0], preferred_element_type=jnp.float32)
        buf[dst, h, 1 + low:1 + high] = stream.astype(jnp.bfloat16).reshape(
            high - low, HALF, channels
        )
        if own:
            skip[h] = jnp.dot(gated, sw[0], preferred_element_type=jnp.float32)

    def last_layer(h):
        gated = gate(1, ((S1M, 1), (S1F, tap_in)), h, 0, strips)
        base = buf[S1M, h, 1:strips + 1].reshape(rows, channels).astype(jnp.float32)
        stream = base + jnp.dot(gated, rw[1], preferred_element_type=jnp.float32)
        stream_ref[h] = stream.astype(jnp.bfloat16)
        total = skip[h] + jnp.dot(gated, sw[1], preferred_element_type=jnp.float32)
        rect_ref[h] = jnp.maximum(total, 0.0).astype(jnp.bfloat16)

    edges, middle = (0, 1), (2,)

    @pl.when(is_mid)
    def _():
        send(M, I, 0, 0, inner)
        send(M, I, 0, 1, outer)
        turn(1)
        for h in range(halves):
            halo_start(M, h)
        send(M, I, 1, 1, outer)
        for part in range(3):
            arrived(O, 0, (part,))
            send(O, F, 0, 2, inner, (part,))
            if part == 1:
                halo_start(O, 0)
        send(M, I, 1, 0, inner)
        arrived(I, 0, edges)
        halo_start(I, 0)
        arrived(I, 0, middle)
        halo_wait(M, 0)
        halo_wait(O, 0)
        halo_wait(I, 0)
        for c in (0, 1, 3, 4):
            weight_copies[c].wait()
        own_taps = ((O, tap_out), (M, 1), (I, tap_in))
        inner_taps = ((M, tap_out), (I, 1), (F, tap_in))
        far_taps = ((I, tap_out), (F, 1))
        first_layer(S1M, M, own_taps, 0, own=True)
        halo_start(S1M, 0)
        for part in range(3):
            arrived(O, 1, (part,))
            send(O, F, 1, 2, inner, (part,))
        halo_start(O, 1)

        def far_blocks(h):
            arrived(F, h, edges)
            halo_start(F, h)
            halo_wait(F, h)
            for part in edges:
                first_layer(S1I, I, inner_taps, h, span=spans(3)[part])
            send(S1I, S1F, h, 3, outer, edges)
            arrived(F, h, middle)
            first_layer(S1I, I, inner_taps, h, span=spans(3)[2])
            send(S1I, S1F, h, 3, outer, middle)
            first_layer(S1F, F, far_taps, h)
            halo_start(S1F, h)

        far_blocks(0)
        arrived(I, 1, edges)
        halo_start(I, 1)
        arrived(I, 1, middle)
        halo_wait(M, 1)
        halo_wait(O, 1)
        halo_wait(I, 1)
        first_layer(S1M, M, own_taps, 1, own=True)
        halo_start(S1M, 1)
        halo_wait(S1M, 0)
        halo_wait(S1F, 0)
        weight_copies[2].wait()
        last_layer(0)
        far_blocks(1)
        halo_wait(S1M, 1)
        halo_wait(S1F, 1)
        last_layer(1)
        for h in range(halves):
            drain(M, I, h, 0, inner)
            drain(M, I, h, 1, outer)
            drain(O, F, h, 2, inner)
            drain(S1I, S1F, h, 3, outer)
            for k in (O, F):
                halo_drain(k, h)

    @pl.when(is_end)
    def _():
        send(M, O, 0, 0, inner)
        turn(1)
        send(M, O, 1, 0, inner)
        for h in range(halves):
            halo_start(M, h)
        for c in (0, 1, 3, 4):
            weight_copies[c].wait()
        for h in range(halves):
            arrived(I, h, edges)
            halo_start(I, h)
            arrived(I, h, middle)
            halo_wait(M, h)
            halo_wait(I, h)
            first_layer(S1M, M, ((M, 1), (I, tap_in)), h, own=True)
            halo_start(S1M, h)
        weight_copies[2].wait()
        for h in range(halves):
            arrived(S1F, h, edges, 3)
            halo_start(S1F, h)
            arrived(S1F, h, middle, 3)
            halo_wait(S1M, h)
            halo_wait(S1F, h)
            last_layer(h)
        for h in range(halves):
            drain(M, O, h, 0, inner)

    for h in range(halves):
        for k in (M, I, S1M, S1F):
            halo_drain(k, h)


def head_kernel(stream_ref, rect_ref, hd_ref, res_ref, out_ref):
    times, strips, channels = res_ref.shape
    rows = times * strips
    r_ids = lax.broadcasted_iota(jnp.int32, (rows, rows), 0)
    c_ids = lax.broadcasted_iota(jnp.int32, (1, rows), 1)
    to_time_major = (
        (c_ids % HALF) * strips + c_ids // HALF == r_ids
    ).astype(jnp.float32).astype(jnp.bfloat16)

    def turned(block):
        return jnp.dot(
            to_time_major, block, preferred_element_type=jnp.float32
        ).astype(jnp.bfloat16)

    res_ref[...] = turned(stream_ref[0]).reshape(times, strips, channels)
    out_ref[...] = jnp.dot(
        turned(rect_ref[0]), hd_ref[...], preferred_element_type=jnp.float32
    ).astype(jnp.bfloat16).reshape(times, strips, -1)


def fused(recording, conv_weight, conv_bias, res_weight, skip_weight, head_weight):
    times, strips, channels = recording.shape
    layers = conv_weight.shape[0]
    halves = times // HALF
    rows = HALF * strips
    pixels = head_weight.shape[1]
    vmem = pl.BlockSpec(memory_space=pltpu.VMEM)
    hbm = pl.BlockSpec(memory_space=pl.ANY)
    weights = conv_weight.reshape(layers, 3, 3 * channels, 2 * channels)
    flat = jax.ShapeDtypeStruct((halves, rows, channels), jnp.bfloat16)
    stream, rectified = pl.pallas_call(
        fused_kernel,
        out_shape=(flat, flat),
        in_specs=[hbm] * 5,
        out_specs=(vmem, vmem),
        scratch_shapes=[
            pltpu.VMEM(recording.shape, jnp.bfloat16),
            pltpu.VMEM(conv_bias.shape, jnp.float32),
            pltpu.VMEM((7, halves, strips + 2, HALF, channels), jnp.bfloat16),
            pltpu.VMEM(weights.shape, jnp.bfloat16),
            pltpu.VMEM(res_weight.shape, jnp.bfloat16),
            pltpu.VMEM(skip_weight.shape, jnp.bfloat16),
            pltpu.VMEM((halves, rows, channels), jnp.float32),
            pltpu.SemaphoreType.DMA((halves,)),
            pltpu.SemaphoreType.DMA((6,)),
            pltpu.SemaphoreType.DMA((4, halves, 3)),
            pltpu.SemaphoreType.DMA((7, halves, 3)),
            pltpu.SemaphoreType.DMA((7, halves, 2)),
            pltpu.SemaphoreType.DMA((7, halves, 2)),
        ],
        compiler_params=pltpu.CompilerParams(
            collective_id=0, has_side_effects=True, vmem_limit_bytes=62 * 2**20
        ),
        cost_estimate=pl.CostEstimate(
            flops=10**10, bytes_accessed=10**7, transcendentals=10**6
        ),
    )(recording, weights, conv_bias, res_weight, skip_weight)
    block = pl.BlockSpec((1, rows, channels), lambda h: (h, 0, 0))
    return pl.pallas_call(
        head_kernel,
        grid=(halves,),
        out_shape=(
            jax.ShapeDtypeStruct((times, strips, channels), jnp.bfloat16),
            jax.ShapeDtypeStruct((times, strips, pixels), jnp.bfloat16),
        ),
        in_specs=[block, block, pl.BlockSpec((channels, pixels), lambda h: (0, 0))],
        out_specs=(
            pl.BlockSpec((HALF, strips, channels), lambda h: (h, 0, 0)),
            pl.BlockSpec((HALF, strips, pixels), lambda h: (h, 0, 0)),
        ),
        compiler_params=pltpu.CompilerParams(vmem_limit_bytes=62 * 2**20),
        cost_estimate=pl.CostEstimate(
            flops=10**9, bytes_accessed=4 * 10**6, transcendentals=0
        ),
    )(stream, rectified, head_weight)


def program(recording, conv_weight, *rest):
    four = lax.axis_size("tm") == 4
    if four and recording.shape[0] == DILATION_SPAN and conv_weight.shape[0] == 2:
        return fused(recording, conv_weight, *rest)
    return local(recording, conv_weight, *rest)


def solution(mesh):
    return jax.shard_map(
        program,
        mesh=mesh,
        in_specs=(P(("groups", "tm"), "fibre", None), P(), P(), P(), P(), P()),
        out_specs=(P(("groups", "tm"), "fibre", None), P(("groups", "tm"), "fibre", None)),
        check_vma=False,
    )
```
